32 devices in a mesh: head: 4 (over z), wide: 8 (over y, x, core).
Axes of the slice: x: 2, y: 2, z: 4, core: 2. Of those that a mesh axis runs over, the one named last changes fastest.
Arguments:
- residual: bfloat16 [1024, 4096], P('head'), may hold values from -150 to 150
- norm_gain: float32 [4096], replicated, may hold values from 0.5 to 1.5
- w_gate: bfloat16 [4096, 7168], P(None, 'wide'), may hold values from -0.09375 to 0.09375
- w_up: bfloat16 [4096, 7168], P(None, 'wide'), may hold values from -0.09375 to 0.09375
- grad_hidden: bfloat16 [1024, 7168], P('head', 'wide'), may hold values from -4 to 4
- grad_out: bfloat16 [1024, 4096], P('head'), may hold values from -4 to 4
- out_proj: bfloat16 [4096, 4096], P('wide', 'head'), may hold values from -0.09375 to 0.09375
- queries: bfloat16 [1024, 4096], P('wide', 'head'), may hold values from -200 to 200
- keys_in: bfloat16 [1024, 512], P('wide', 'head'), may hold values from -4 to 4
- values_in: bfloat16 [1024, 512], P('wide', 'head'), may hold values from -6 to 6
- doc_ids: int32 [1024], replicated, may hold values from 0 to 3, never falling along the last dimension, each value on 1 to 768 neighbouring positions
Outputs:
- grad_resid: bfloat16 [1024, 4096], P('head')
- grad_gain: float32 [4096], replicated
- grad_gate: bfloat16 [4096, 7168], P('head', 'wide')
- grad_up: bfloat16 [4096, 7168], P('head', 'wide')
- grad_proj: bfloat16 [4096, 4096], P('wide', 'head')
- grad_query: bfloat16 [1024, 4096], P('wide', 'head')
- grad_key: bfloat16 [1024, 512], P('wide', 'head')
- grad_value: bfloat16 [1024, 512], P('wide', 'head')
The draws below stay inside these ranges and needn't reach their ends.
Inputs may be any that keep to these rules, and one draw needn't show every extreme that they name: `doc_ids`: document ids never fall along the tokens; each document holds at most 768 tokens, and one holds exactly that many.
All inputs are finite; a program needn't handle non-finite values.
Results may differ from the reference program's by a relative error of at most 0.019.
Values may be sent and summed in bfloat16 or wider, within the bound.
A program may use at most 192 MiB of HBM per device.

```python
import math
import jax
import jax.numpy as jnp
import numpy as np
from jax import lax

D = 4096
HD = 128
QPK = 8
KVH = 4
HQ = 32
FF = 7168
TOK_ATT = 128
TOKENS = 1024
TOK_MLP = 256
N_HEAD = 4
N_WIDE = 8


def key_base(key):
    return jnp.clip(jax.random.normal(key, (TOKENS, KVH, HD), jnp.float32), -4.0, 4.0)


def draw_keys_in(key, part):
    base = key_base(key)
    return base.reshape(TOKENS, KVH * HD).astype(jnp.bfloat16)


def draw_queries(key, part):
    key = jax.random.fold_in(key, 11)
    own = jnp.clip(jax.random.normal(key, (TOKENS, KVH, QPK, HD), jnp.float32), -4.0, 4.0)
    return jnp.clip(own, -200.0, 200.0).reshape(TOKENS, KVH * QPK * HD).astype(jnp.bfloat16)


def draw_residual(key, part):
    key = jax.random.fold_in(key, 5)
    key_vals, key_rows, key_cols = jax.random.split(key, 3)
    row_scale = jnp.exp(jax.random.uniform(key_rows, (TOKENS, 1), jnp.float32, 0.0, math.log(10.0)))
    col_scale = jnp.exp(jax.random.uniform(key_cols, (1, D), jnp.float32, math.log(0.3), math.log(3.0)))
    base = jnp.clip(jax.random.normal(key_vals, (TOKENS, D), jnp.float32), -4.0, 4.0)
    return jnp.clip(base * row_scale * col_scale, -150.0, 150.0).astype(jnp.bfloat16)


def levels(stream_key, dims, shards, low, top_value):
    level = 1.0
    for position, blocks in shards:
        heights = jax.random.uniform(jax.random.fold_in(jax.random.fold_in(stream_key, 6), position), (blocks,), jnp.float32, low / len(shards), top_value / len(shards))
        level = level * jnp.repeat(jnp.exp(heights), dims[position] // blocks).reshape((-1,) + (1,) * (len(dims) - 1 - position))
    return level


def profile(number_of, total, bound, skew):
    weights = [(1 << 20) // math.isqrt(grade ** skew) + 1 for grade in range(2, number_of + 1)]
    surplus, holding = total - bound - (number_of - 1), [1] * (number_of - 1)
    while surplus > 0:
        free = [i for i in range(number_of - 1) if holding[i] < bound]
        pool, left = sum([weights[i] for i in free]), surplus
        for i in free:
            extra = min(bound - holding[i], max(1, left * weights[i] // pool), surplus)
            holding[i] = holding[i] + extra
            surplus = surplus - extra
    return np.array([bound] + holding)


def uneven_parts(key, number_of, total, bound, skew):
    if number_of == 2:
        one = jax.random.randint(key, (), max(1, total - bound), min(bound, total - 1) + 1)
        return jnp.stack([one, total - one])
    lengths = jnp.asarray(profile(number_of, total, bound, skew), jnp.int32)
    twos = (number_of - 1) // 2
    giver, sink = lengths[1:1 + 2 * twos:2], lengths[2:2 + 2 * twos:2]
    margin = jnp.minimum(giver - 1, bound - sink)
    passed = jax.random.randint(jax.random.fold_in(key, 1), (twos,), 0, 1 << 20) % (margin + 1)
    lengths = lengths.at[1:1 + 2 * twos:2].set(giver - passed).at[2:2 + 2 * twos:2].set(sink + passed)
    return lengths[jax.random.permutation(jax.random.fold_in(key, 2), number_of)]


def scatter_about(key, dims, scale, most, shards=(), kind=jnp.bfloat16):
    drawn = scale * jax.random.normal(key, dims, jnp.float32)
    if shards:
        drawn = drawn * levels(key, dims, shards, -0.22, 0.18)
    return jnp.clip(drawn, -most, most).astype(kind)


def setup_inputs(seed: int = 0) -> dict:
    key_of = jax.random.split(jax.random.key(seed), 12)
    residual = draw_residual(jax.random.fold_in(key_of[11], 71), 0)
    norm_gain = jnp.clip(1.0 + 0.1 * jax.random.normal(key_of[1], (D,), jnp.float32), 0.5, 1.5)
    w_gate = scatter_about(key_of[2], (D, FF), D ** -0.5, 0.09375, ((1, 8),))
    w_up = scatter_about(key_of[3], (D, FF), D ** -0.5, 0.09375, ((1, 8),))
    grad_hidden = scatter_about(key_of[4], (TOKENS, FF), 0.25, 4.0, ((0, 4), (1, 8)))
    grad_out = scatter_about(key_of[5], (TOKENS, D), 0.3, 4.0, ((0, 4),))
    out_proj = scatter_about(key_of[6], (D, HQ * HD), (HQ * HD) ** -0.5, 0.09375, ((0, 8), (1, 4)))
    queries = draw_queries(jax.random.fold_in(key_of[11], 71), 0)
    keys_in = draw_keys_in(jax.random.fold_in(key_of[11], 71), 0)
    values_in = scatter_about(key_of[9], (TOKENS, KVH * HD), 1.0, 6.0, ((0, 8), (1, 4)))
    doc_ids = jnp.searchsorted(jnp.cumsum(uneven_parts(key_of[10], 4, TOKENS, TOKENS * 3 // 4, 1)), jnp.arange(TOKENS), side="right").astype(jnp.int32)
    return {"residual": residual, "norm_gain": norm_gain, "w_gate": w_gate, "w_up": w_up, "grad_hidden": grad_hidden, "grad_out": grad_out, "out_proj": out_proj, "queries": queries, "keys_in": keys_in, "values_in": values_in, "doc_ids": doc_ids}


EPSILON = 1e-05

def reference(residual, norm_gain, w_gate, w_up, grad_hidden, grad_out, out_proj, queries, keys_in, values_in, doc_ids):
    resid_f = residual.astype(jnp.float32)
    inv_rms = lax.rsqrt(lax.optimization_barrier(jnp.mean(resid_f * resid_f, axis=-1, keepdims=True)) + EPSILON)
    normed_f = resid_f * inv_rms
    normed = (normed_f * norm_gain).astype(jnp.bfloat16)
    gate_pre = jnp.dot(normed, w_gate, preferred_element_type=jnp.float32)
    up_pre = jnp.dot(normed, w_up, preferred_element_type=jnp.float32)
    sigma = jax.nn.sigmoid(gate_pre)
    grad_h = grad_hidden.astype(jnp.float32)
    grad_g = (grad_h * up_pre * sigma * (1.0 + gate_pre * (1.0 - sigma))).astype(jnp.bfloat16)
    grad_u = (grad_h * gate_pre * sigma).astype(jnp.bfloat16)
    grad_norm = jnp.dot(grad_g, w_gate.T, preferred_element_type=jnp.float32) + jnp.dot(grad_u, w_up.T, preferred_element_type=jnp.float32)
    both_grads = jnp.concatenate([grad_g, grad_u], axis=1)

    def weight_block(summed, pair):
        rows_in, grads = pair
        term = jnp.dot(rows_in.T, grads, preferred_element_type=jnp.float32)
        return (summed + lax.optimization_barrier(term.astype(jnp.bfloat16)).astype(jnp.float32), None)
    weight_sums, _ = lax.scan(weight_block, jnp.zeros((D, 2 * FF), jnp.float32), (normed.reshape(N_HEAD, TOK_MLP, D), both_grads.reshape(N_HEAD, TOK_MLP, 2 * FF)))
    grad_gate = weight_sums[:, :FF].astype(jnp.bfloat16)
    grad_up = weight_sums[:, FF:].astype(jnp.bfloat16)
    grad_gain = lax.optimization_barrier(jnp.sum(grad_norm * normed_f, axis=0))
    scaled = grad_norm * norm_gain
    mean_term = lax.optimization_barrier(jnp.mean(scaled * normed_f, axis=-1, keepdims=True))
    grad_resid = (grad_out.astype(jnp.float32) + inv_rms * (scaled - normed_f * mean_term)).astype(jnp.bfloat16)
    grad_heads = jnp.dot(grad_resid, out_proj, preferred_element_type=jnp.float32).astype(jnp.bfloat16)
    positions = jnp.arange(TOKENS, dtype=jnp.int32)
    visible = (doc_ids[:, None] == doc_ids[None, :]) & (positions[None, :] <= positions[:, None])
    score_scale = 1.0 / math.sqrt(HD)

    def one_group(operands):
        query_grp, key_grp, value_grp, dhead_grp = operands
        query32 = query_grp.astype(jnp.float32)
        key32 = key_grp.astype(jnp.float32)
        value32 = value_grp.astype(jnp.float32)
        dhead32 = dhead_grp.astype(jnp.float32)
        scores = jnp.einsum('thd,sd->hts', query32, key32) * score_scale
        scores = jnp.where(visible[None], scores, -1e+30)
        top = lax.optimization_barrier(jnp.max(scores, axis=-1, keepdims=True))
        expo = jnp.exp(scores - top)
        prob = expo / lax.optimization_barrier(jnp.sum(expo, axis=-1, keepdims=True))
        prob_b = prob.astype(jnp.bfloat16).astype(jnp.float32)
        outs = jnp.einsum('hts,sd->thd', prob_b, value32).astype(jnp.bfloat16)
        dprob = jnp.einsum('thd,sd->hts', dhead32, value32)
        delta = lax.optimization_barrier(jnp.sum(prob * dprob, axis=-1, keepdims=True))
        dscore = (prob * (dprob - delta) * score_scale).astype(jnp.bfloat16).astype(jnp.float32)
        grad_q = jnp.einsum('hts,sd->thd', dscore, key32).astype(jnp.bfloat16)
        grad_k = jnp.einsum('hts,thd->sd', dscore, query32).astype(jnp.bfloat16)
        grad_v = jnp.einsum('hts,thd->sd', prob_b, dhead32).astype(jnp.bfloat16)
        return (outs, grad_q, grad_k, grad_v)
    query_groups = queries.reshape(TOKENS, KVH, QPK, HD).transpose(1, 0, 2, 3)
    key_groups = keys_in.reshape(TOKENS, KVH, HD).transpose(1, 0, 2)
    value_groups = values_in.reshape(TOKENS, KVH, HD).transpose(1, 0, 2)
    dhead_groups = grad_heads.reshape(TOKENS, KVH, QPK, HD).transpose(1, 0, 2, 3)
    outs, grad_q, grad_k, grad_v = lax.map(one_group, (query_groups, key_groups, value_groups, dhead_groups))
    attn_out = outs.transpose(1, 0, 2, 3).reshape(TOKENS, HQ * HD)
    grad_query = grad_q.transpose(1, 0, 2, 3).reshape(TOKENS, HQ * HD)
    grad_key = grad_k.transpose(1, 0, 2).reshape(TOKENS, KVH * HD)
    grad_value = grad_v.transpose(1, 0, 2).reshape(TOKENS, KVH * HD)

    def proj_block(summed, pair):
        resid_blk, out_blk = pair
        term = jnp.dot(resid_blk.T, out_blk, preferred_element_type=jnp.float32)
        return (summed + lax.optimization_barrier(term.astype(jnp.bfloat16)).astype(jnp.float32), None)
    proj_sum, _ = lax.scan(proj_block, jnp.zeros((D, HQ * HD), jnp.float32), (grad_resid.reshape(N_WIDE, TOK_ATT, D), attn_out.reshape(N_WIDE, TOK_ATT, HQ * HD)))
    grad_proj = proj_sum.astype(jnp.bfloat16)
    return (grad_resid, grad_gain, grad_gate, grad_up, grad_proj, grad_query, grad_key, grad_value)
```

```python
import functools
import math

import jax
import jax.numpy as jnp
from jax import lax
from jax.experimental import pallas as pl
from jax.experimental.pallas import tpu as pltpu
from jax.sharding import PartitionSpec as P

EPSILON = 1e-05
MESH = pl.DeviceIdType.MESH
ANY = pl.BlockSpec(memory_space=pl.ANY)
VMEM = pl.BlockSpec(memory_space=pltpu.VMEM)


def enter(groups):
    barrier = pltpu.get_barrier_semaphore()
    total = 0
    for axis, n in groups:
        me = lax.axis_index(axis)
        for k in range(1, n):
            pl.semaphore_signal(
                barrier, inc=1, device_id={axis: lax.rem(me + k, n)}, device_id_type=MESH
            )
        total += n - 1
    pl.semaphore_wait(barrier, total)


def part(ref, dim, index, size):
    start = pl.multiple_of(index * size, size)
    if dim == 0:
        return ref.at[pl.ds(start, size)]
    return ref.at[:, pl.ds(start, size)]


def params(collective_id):
    return pltpu.CompilerParams(
        collective_id=collective_id, has_side_effects=True, vmem_limit_bytes=32 * 1024 * 1024
    )


def scatter_sum_kernel(axis, n, dim, src, out, held, send_sem, recv_sem, own_sem):
    me = lax.axis_index(axis)
    size = out.shape[dim]
    own = pltpu.make_async_copy(part(src, dim, me, size), held.at[0], own_sem)
    own.start()
    enter([(axis, n)])
    copies = []
    for k in range(1, n):
        peer = lax.rem(me + k, n)
        copies.append(
            pltpu.make_async_remote_copy(
                src_ref=part(src, dim, peer, size),
                dst_ref=held.at[k],
                send_sem=send_sem.at[k],
                recv_sem=recv_sem.at[k],
                device_id={axis: peer},
                device_id_type=MESH,
            )
        )
        copies[-1].start()
    own.wait()
    for copy in copies:
        copy.wait()
    step = 32

    @pl.loop(0, out.shape[0] // step)
    def _(i):
        rows = pl.ds(pl.multiple_of(i * step, step), step)
        total = held[0, rows].astype(jnp.float32)
        for k in range(1, n):
            total = total + held[k, rows].astype(jnp.float32)
        out[rows] = total.astype(out.dtype)


def scatter_sum(x, axis, dim, collective_id):
    n = lax.axis_size(axis)
    shape = list(x.shape)
    shape[dim] //= n
    return pl.pallas_call(
        functools.partial(scatter_sum_kernel, axis, n, dim),
        out_shape=jax.ShapeDtypeStruct(tuple(shape), x.dtype),
        in_specs=[ANY],
        out_specs=VMEM,
        scratch_shapes=[
            pltpu.VMEM((n, *shape), x.dtype),
            pltpu.SemaphoreType.DMA((n,)),
            pltpu.SemaphoreType.DMA((n,)),
            pltpu.SemaphoreType.DMA,
        ],
        compiler_params=params(collective_id),
    )(x)


def gather_kernel(plan, *refs):
    count = len(plan)
    srcs, outs = refs[:count], refs[count : 2 * count]
    sems = refs[2 * count :]
    groups = []
    for axis, n, _ in plan:
        if (axis, n) not in groups:
            groups.append((axis, n))
    owns = []
    for i, (axis, n, dim) in enumerate(plan):
        me = lax.axis_index(axis)
        own = pltpu.make_async_copy(
            srcs[i], part(outs[i], dim, me, srcs[i].shape[dim]), sems[3 * i + 2]
        )
        own.start()
        owns.append(own)
    enter(groups)
    copies = []
    for i, (axis, n, dim) in enumerate(plan):
        me = lax.axis_index(axis)
        for k in range(1, n):
            copy = pltpu.make_async_remote_copy(
                src_ref=srcs[i],
                dst_ref=part(outs[i], dim, me, srcs[i].shape[dim]),
                send_sem=sems[3 * i].at[k],
                recv_sem=sems[3 * i + 1].at[k],
                device_id={axis: lax.rem(me + k, n)},
                device_id_type=MESH,
            )
            copy.start()
            copies.append(copy)
    for own in owns:
        own.wait()
    for copy in copies:
        copy.wait()


def gather(arrays, axes_dims, collective_id):
    plan, outs, scratch = [], [], []
    for x, (axis, dim) in zip(arrays, axes_dims):
        n = lax.axis_size(axis)
        plan.append((axis, n, dim))
        shape = list(x.shape)
        shape[dim] *= n
        outs.append(jax.ShapeDtypeStruct(tuple(shape), x.dtype))
        scratch += [
            pltpu.SemaphoreType.DMA((n,)),
            pltpu.SemaphoreType.DMA((n,)),
            pltpu.SemaphoreType.DMA,
        ]
    return pl.pallas_call(
        functools.partial(gather_kernel, plan),
        out_shape=outs,
        in_specs=[ANY] * len(arrays),
        out_specs=[ANY] * len(arrays),
        scratch_shapes=scratch,
        compiler_params=params(collective_id),
    )(*arrays)


def shifted(x, axis, n, k):
    return lax.ppermute(x, axis, [(i, (i + k) % n) for i in range(n)])


def local(
    residual,
    norm_gain,
    w_gate,
    w_up,
    grad_hidden,
    grad_out,
    out_proj,
    queries,
    keys_in,
    values_in,
    doc_ids,
):
    heads_n = lax.axis_size("head")
    wide_n = lax.axis_size("wide")
    head_at = lax.axis_index("head")
    wide_at = lax.axis_index("wide")
    tok_mlp, width = residual.shape
    cols_wide = width // wide_n
    cols_head = width // heads_n
    contract_last = (((1,), (1,)), ((), ()))
    contract_first = (((0,), (0,)), ((), ()))
    tok_att = queries.shape[0]
    head_dim = keys_in.shape[1]
    per_kv = queries.shape[1] // head_dim
    score_scale = 1.0 / math.sqrt(head_dim)

    kv_all = lax.all_gather(
        jnp.concatenate([keys_in, values_in], axis=1), "wide", axis=0, tiled=True
    )
    keys_all, values_all = kv_all[:, :head_dim], kv_all[:, head_dim:]

    resid_f = residual.astype(jnp.float32)
    inv_rms = lax.rsqrt(jnp.mean(resid_f * resid_f, axis=-1, keepdims=True) + EPSILON)
    normed = (resid_f * inv_rms * norm_gain).astype(jnp.bfloat16)

    def normed_cols(owner):
        return lax.dynamic_slice_in_dim(normed, owner * cols_head, cols_head, 1)

    normed_parts = [normed_cols(head_at)]
    for k in range(1, heads_n):
        normed_parts.append(
            shifted(normed_cols(lax.rem(head_at + k, heads_n)), "head", heads_n, k)
        )

    gate_pre = jnp.dot(normed, w_gate, preferred_element_type=jnp.float32)
    up_pre = jnp.dot(normed, w_up, preferred_element_type=jnp.float32)
    sigma = jax.nn.sigmoid(gate_pre)
    grad_h = grad_hidden.astype(jnp.float32)
    grad_g = (grad_h * up_pre * sigma * (1.0 + gate_pre * (1.0 - sigma))).astype(jnp.bfloat16)
    grad_u = (grad_h * gate_pre * sigma).astype(jnp.bfloat16)
    partial_norm = lax.dot_general(
        grad_g, w_gate, contract_last, preferred_element_type=jnp.float32
    )
    partial_norm = partial_norm + lax.dot_general(
        grad_u, w_up, contract_last, preferred_element_type=jnp.float32
    )
    gate_parts, up_parts = [grad_g], [grad_u]
    for k in range(1, heads_n):
        gate_parts.append(shifted(grad_g, "head", heads_n, k))
        up_parts.append(shifted(grad_u, "head", heads_n, k))

    grad_norm = scatter_sum(partial_norm.astype(jnp.bfloat16), "wide", 1, 1).astype(jnp.float32)
    resid_own = lax.dynamic_slice_in_dim(residual, wide_at * cols_wide, cols_wide, 1)
    normed_own = resid_own.astype(jnp.float32) * inv_rms
    gain_own = lax.dynamic_slice_in_dim(norm_gain, wide_at * cols_wide, cols_wide, 0)
    out_own = lax.dynamic_slice_in_dim(grad_out, wide_at * cols_wide, cols_wide, 1)
    product = grad_norm * normed_own
    stats = jnp.concatenate([jnp.sum(product * gain_own, axis=1), jnp.sum(product, axis=0)])
    stat_len = -(-stats.shape[0] // 1024) * 1024
    stats = jnp.pad(stats, (0, stat_len - stats.shape[0])).reshape(stat_len // 128, 128)
    (stats_all,) = gather([stats], [("wide", 0)], 2)
    stats_all = stats_all.reshape(wide_n, stat_len)
    mean_term = (jnp.sum(stats_all[:, :tok_mlp], axis=0) / width)[:, None]
    gain_part = stats_all[:, tok_mlp : tok_mlp + cols_wide].reshape(width // 128, 128)
    resid_grad = (
        out_own.astype(jnp.float32) + inv_rms * (grad_norm * gain_own - normed_own * mean_term)
    ).astype(jnp.bfloat16)
    resid_cols, gain_all = gather([resid_grad, gain_part], [("head", 0), ("head", 0)], 3)
    grad_gain = jnp.sum(gain_all.reshape(heads_n, width), axis=0)
    grad_resid = lax.all_gather(resid_grad, "wide", axis=1, tiled=True)

    tok_total = keys_all.shape[0]
    q_offset = wide_at * tok_att
    positions = jnp.arange(tok_total, dtype=jnp.int32)
    q_pos = q_offset + jnp.arange(tok_att, dtype=jnp.int32)
    q_docs = lax.dynamic_slice_in_dim(doc_ids, q_offset, tok_att, 0)
    visible = (q_docs[:, None] == doc_ids[None, :]) & (positions[None, :] <= q_pos[:, None])
    query3 = queries.reshape(tok_att, per_kv, head_dim)
    scores = (
        jnp.einsum("thd,sd->hts", query3, keys_all, preferred_element_type=jnp.float32)
        * score_scale
    )
    scores = jnp.where(visible[None], scores, -1e30)
    top = jnp.max(scores, axis=-1, keepdims=True)
    expo = jnp.exp(scores - top)
    prob = expo / jnp.sum(expo, axis=-1, keepdims=True)
    prob_b = prob.astype(jnp.bfloat16)
    attn_out = jnp.einsum("hts,sd->thd", prob_b, values_all, preferred_element_type=jnp.float32)
    attn_out = attn_out.astype(jnp.bfloat16).reshape(tok_att, per_kv * head_dim)
    attn_all = lax.all_gather(attn_out, "wide", axis=0, tiled=True)

    heads_part = jnp.dot(resid_cols, out_proj, preferred_element_type=jnp.float32)
    grad_heads = scatter_sum(heads_part.astype(jnp.bfloat16), "wide", 0, 4)
    grad_heads = grad_heads.reshape(tok_att, per_kv, head_dim)
    dprob = jnp.einsum("thd,sd->hts", grad_heads, values_all, preferred_element_type=jnp.float32)
    delta = jnp.sum(prob * dprob, axis=-1, keepdims=True)
    dscore = (prob * (dprob - delta) * score_scale).astype(jnp.bfloat16)
    grad_query = jnp.einsum("hts,sd->thd", dscore, keys_all, preferred_element_type=jnp.float32)
    grad_query = grad_query.astype(jnp.bfloat16).reshape(tok_att, per_kv * head_dim)
    key_part = jnp.einsum("hts,thd->sd", dscore, query3, preferred_element_type=jnp.float32)
    value_part = jnp.einsum("hts,thd->sd", prob_b, grad_heads, preferred_element_type=jnp.float32)
    kv_sum = scatter_sum(
        jnp.concatenate([key_part, value_part], axis=1).astype(jnp.bfloat16), "wide", 0, 5
    )

    grad_proj = lax.dot_general(
        resid_cols, attn_all, contract_first, preferred_element_type=jnp.float32
    ).astype(jnp.bfloat16)
    normed_all = jnp.concatenate(normed_parts, axis=0)
    grad_gate = lax.dot_general(
        normed_all,
        jnp.concatenate(gate_parts, axis=0),
        contract_first,
        preferred_element_type=jnp.float32,
    ).astype(jnp.bfloat16)
    grad_up = lax.dot_general(
        normed_all,
        jnp.concatenate(up_parts, axis=0),
        contract_first,
        preferred_element_type=jnp.float32,
    ).astype(jnp.bfloat16)
    return (
        grad_resid,
        grad_gain,
        grad_gate,
        grad_up,
        grad_proj,
        grad_query,
        kv_sum[:, :head_dim],
        kv_sum[:, head_dim:],
    )


def solution(mesh):
    return jax.shard_map(
        local,
        mesh=mesh,
        in_specs=(
            P("head", None),
            P(),
            P(None, "wide"),
            P(None, "wide"),
            P("head", "wide"),
            P("head", None),
            P("wide", "head"),
            P("wide", "head"),
            P("wide", "head"),
            P("wide", "head"),
            P(),
        ),
        out_specs=(
            P("head", None),
            P(),
            P("head", "wide"),
            P("head", "wide"),
            P("wide", "head"),
            P("wide", "head"),
            P("wide", "head"),
            P("wide", "head"),
        ),
        check_vma=False,
    )
```

```python
import functools
import math

import jax
import jax.numpy as jnp
from jax import lax
from jax.experimental import pallas as pl
from jax.experimental.pallas import tpu as pltpu
from jax.sharding import PartitionSpec as P

EPSILON = 1e-05
MESH = pl.DeviceIdType.MESH
ANY = pl.BlockSpec(memory_space=pl.ANY)
VMEM = pl.BlockSpec(memory_space=pltpu.VMEM)


def enter(groups):
    barrier = pltpu.get_barrier_semaphore()
    total = 0
    for axis, n in groups:
        me = lax.axis_index(axis)
        for k in range(1, n):
            pl.semaphore_signal(
                barrier, inc=1, device_id={axis: lax.rem(me + k, n)}, device_id_type=MESH
            )
        total += n - 1
    pl.semaphore_wait(barrier, total)


def part(ref, dim, index, size):
    start = pl.multiple_of(index * size, size)
    if dim == 0:
        return ref.at[pl.ds(start, size)]
    return ref.at[:, pl.ds(start, size)]


def params(collective_id):
    return pltpu.CompilerParams(
        collective_id=collective_id, has_side_effects=True, vmem_limit_bytes=32 * 1024 * 1024
    )


def scatter_sum_kernel(axis, n, dim, src, out, held, send_sem, recv_sem, own_sem):
    me = lax.axis_index(axis)
    size = out.shape[dim]
    own = pltpu.make_async_copy(part(src, dim, me, size), held.at[0], own_sem)
    own.start()
    enter([(axis, n)])
    copies = []
    for k in range(1, n):
        peer = lax.rem(me + k, n)
        copies.append(
            pltpu.make_async_remote_copy(
                src_ref=part(src, dim, peer, size),
                dst_ref=held.at[k],
                send_sem=send_sem.at[k],
                recv_sem=recv_sem.at[k],
                device_id={axis: peer},
                device_id_type=MESH,
            )
        )
        copies[-1].start()
    own.wait()
    for copy in copies:
        copy.wait()
    step = 32

    @pl.loop(0, out.shape[0] // step)
    def _(i):
        rows = pl.ds(pl.multiple_of(i * step, step), step)
        total = held[0, rows].astype(jnp.float32)
        for k in range(1, n):
            total = total + held[k, rows].astype(jnp.float32)
        out[rows] = total.astype(out.dtype)


def scatter_sum(x, axis, dim, collective_id):
    n = lax.axis_size(axis)
    shape = list(x.shape)
    shape[dim] //= n
    return pl.pallas_call(
        functools.partial(scatter_sum_kernel, axis, n, dim),
        out_shape=jax.ShapeDtypeStruct(tuple(shape), x.dtype),
        in_specs=[ANY],
        out_specs=VMEM,
        scratch_shapes=[
            pltpu.VMEM((n, *shape), x.dtype),
            pltpu.SemaphoreType.DMA((n,)),
            pltpu.SemaphoreType.DMA((n,)),
            pltpu.SemaphoreType.DMA,
        ],
        compiler_params=params(collective_id),
    )(x)


def pair_scatter_kernel(
    axis, n, dim, src, out, own, near, sums, far, near_sems, far_sems, own_sems
):
    pairs = n // 2
    me = lax.axis_index(axis)
    chip, core = me // 2, lax.rem(me, 2)
    partner = chip * 2 + 1 - core
    size = out.shape[dim]
    order = list(range(1, pairs)) + [0]
    chips = [lax.rem(chip + k, pairs) for k in range(pairs)]
    owns = {}
    for k in order:
        owns[k] = pltpu.make_async_copy(
            part(src, dim, chips[k] * 2 + core, size), own.at[k], own_sems.at[k]
        )
        owns[k].start()
    barrier = pltpu.get_barrier_semaphore()
    for k in range(pairs):
        peer = partner if k == 0 else chips[k] * 2 + core
        pl.semaphore_signal(barrier, inc=1, device_id={axis: peer}, device_id_type=MESH)
    pl.semaphore_wait(barrier, pairs)
    nears, fars = {}, {}
    for k in order:
        nears[k] = pltpu.make_async_remote_copy(
            src_ref=part(src, dim, chips[k] * 2 + 1 - core, size),
            dst_ref=near.at[k],
            send_sem=near_sems.at[0, k],
            recv_sem=near_sems.at[1, k],
            device_id={axis: partner},
            device_id_type=MESH,
        )
        nears[k].start()
    step = 32
    for k in order:
        owns[k].wait()
        nears[k].wait()
        if k == 0:
            continue

        @pl.loop(0, out.shape[0] // step)
        def _(i):
            rows = pl.ds(pl.multiple_of(i * step, step), step)
            total = own[k, rows].astype(jnp.float32) + near[k, rows].astype(jnp.float32)
            sums[k, rows] = total.astype(sums.dtype)

        fars[k] = pltpu.make_async_remote_copy(
            src_ref=sums.at[k],
            dst_ref=far.at[k],
            send_sem=far_sems.at[0, k],
            recv_sem=far_sems.at[1, k],
            device_id={axis: chips[k] * 2 + core},
            device_id_type=MESH,
        )
        fars[k].start()
    for k in range(1, pairs):
        fars[k].wait()

    @pl.loop(0, out.shape[0] // step)
    def _(i):
        rows = pl.ds(pl.multiple_of(i * step, step), step)
        total = own[0, rows].astype(jnp.float32) + near[0, rows].astype(jnp.float32)
        for k in range(1, pairs):
            total = total + far[k, rows].astype(jnp.float32)
        out[rows] = total.astype(out.dtype)


def pair_scatter_sum(x, axis, dim, collective_id):
    n = lax.axis_size(axis)
    shape = list(x.shape)
    shape[dim] //= n
    held = pltpu.VMEM((n // 2, *shape), x.dtype)
    return pl.pallas_call(
        functools.partial(pair_scatter_kernel, axis, n, dim),
        out_shape=jax.ShapeDtypeStruct(tuple(shape), x.dtype),
        in_specs=[ANY],
        out_specs=VMEM,
        scratch_shapes=[
            held,
            held,
            held,
            held,
            pltpu.SemaphoreType.DMA((2, n // 2)),
            pltpu.SemaphoreType.DMA((2, n // 2)),
            pltpu.SemaphoreType.DMA((n // 2,)),
        ],
        compiler_params=params(collective_id),
    )(x)


def gather_kernel(plan, *refs):
    count = len(plan)
    srcs, outs = refs[:count], refs[count : 2 * count]
    sems = refs[2 * count :]
    groups = []
    for axis, n, _ in plan:
        if (axis, n) not in groups:
            groups.append((axis, n))
    owns = []
    for i, (axis, n, dim) in enumerate(plan):
        me = lax.axis_index(axis)
        own = pltpu.make_async_copy(
            srcs[i], part(outs[i], dim, me, srcs[i].shape[dim]), sems[3 * i + 2]
        )
        own.start()
        owns.append(own)
    enter(groups)
    copies = []
    for i, (axis, n, dim) in enumerate(plan):
        me = lax.axis_index(axis)
        for k in range(1, n):
            copy = pltpu.make_async_remote_copy(
                src_ref=srcs[i],
                dst_ref=part(outs[i], dim, me, srcs[i].shape[dim]),
                send_sem=sems[3 * i].at[k],
                recv_sem=sems[3 * i + 1].at[k],
                device_id={axis: lax.rem(me + k, n)},
                device_id_type=MESH,
            )
            copy.start()
            copies.append(copy)
    for own in owns:
        own.wait()
    for copy in copies:
        copy.wait()


def gather(arrays, axes_dims, collective_id):
    plan, outs, scratch = [], [], []
    for x, (axis, dim) in zip(arrays, axes_dims):
        n = lax.axis_size(axis)
        plan.append((axis, n, dim))
        shape = list(x.shape)
        shape[dim] *= n
        outs.append(jax.ShapeDtypeStruct(tuple(shape), x.dtype))
        scratch += [
            pltpu.SemaphoreType.DMA((n,)),
            pltpu.SemaphoreType.DMA((n,)),
            pltpu.SemaphoreType.DMA,
        ]
    return pl.pallas_call(
        functools.partial(gather_kernel, plan),
        out_shape=outs,
        in_specs=[ANY] * len(arrays),
        out_specs=[ANY] * len(arrays),
        scratch_shapes=scratch,
        compiler_params=params(collective_id),
    )(*arrays)


def shifted(x, axis, n, k):
    return lax.ppermute(x, axis, [(i, (i + k) % n) for i in range(n)])


def local(
    residual,
    norm_gain,
    w_gate,
    w_up,
    grad_hidden,
    grad_out,
    out_proj,
    queries,
    keys_in,
    values_in,
    doc_ids,
):
    heads_n = lax.axis_size("head")
    wide_n = lax.axis_size("wide")
    head_at = lax.axis_index("head")
    wide_at = lax.axis_index("wide")
    tok_mlp, width = residual.shape
    cols_wide = width // wide_n
    cols_head = width // heads_n
    contract_last = (((1,), (1,)), ((), ()))
    contract_first = (((0,), (0,)), ((), ()))
    tok_att = queries.shape[0]
    head_dim = keys_in.shape[1]
    per_kv = queries.shape[1] // head_dim
    score_scale = 1.0 / math.sqrt(head_dim)

    keys_all, values_all = gather([keys_in, values_in], [("wide", 0), ("wide", 0)], 6)

    resid_f = residual.astype(jnp.float32)
    inv_rms = lax.rsqrt(jnp.mean(resid_f * resid_f, axis=-1, keepdims=True) + EPSILON)
    normed = (resid_f * inv_rms * norm_gain).astype(jnp.bfloat16)

    core = lax.rem(wide_at, 2)
    cols_half = cols_head // 2

    def normed_cols(owner):
        return lax.dynamic_slice_in_dim(normed, owner * cols_head + core * cols_half, cols_half, 1)

    normed_parts = [normed_cols(head_at)]
    for k in range(1, heads_n):
        normed_parts.append(
            shifted(normed_cols(lax.rem(head_at + k, heads_n)), "head", heads_n, k)
        )

    gate_pre = jnp.dot(normed, w_gate, preferred_element_type=jnp.float32)
    up_pre = jnp.dot(normed, w_up, preferred_element_type=jnp.float32)
    sigma = jax.nn.sigmoid(gate_pre)
    grad_h = grad_hidden.astype(jnp.float32)
    grad_g = (grad_h * up_pre * sigma * (1.0 + gate_pre * (1.0 - sigma))).astype(jnp.bfloat16)
    grad_u = (grad_h * gate_pre * sigma).astype(jnp.bfloat16)
    partial_norm = lax.dot_general(
        grad_g, w_gate, contract_last, preferred_element_type=jnp.float32
    )
    partial_norm = partial_norm + lax.dot_general(
        grad_u, w_up, contract_last, preferred_element_type=jnp.float32
    )
    both_grads = jnp.concatenate([grad_g, grad_u], axis=1)
    grads_parts = [both_grads]
    for k in range(1, heads_n):
        grads_parts.append(shifted(both_grads, "head", heads_n, k))

    partial_norm, normed_parts = lax.optimization_barrier(
        (partial_norm.astype(jnp.bfloat16), normed_parts)
    )
    grad_norm = pair_scatter_sum(partial_norm, "wide", 1, 1).astype(jnp.float32)
    resid_own = lax.dynamic_slice_in_dim(residual, wide_at * cols_wide, cols_wide, 1)
    normed_own = resid_own.astype(jnp.float32) * inv_rms
    gain_own = lax.dynamic_slice_in_dim(norm_gain, wide_at * cols_wide, cols_wide, 0)
    out_own = lax.dynamic_slice_in_dim(grad_out, wide_at * cols_wide, cols_wide, 1)
    product = grad_norm * normed_own
    stats = jnp.concatenate([jnp.sum(product * gain_own, axis=1), jnp.sum(product, axis=0)])
    stat_len = -(-stats.shape[0] // 1024) * 1024
    stats = jnp.pad(stats, (0, stat_len - stats.shape[0])).reshape(stat_len // 128, 128)
    (stats_all,) = gather([stats], [("wide", 0)], 2)
    stats_all = stats_all.reshape(wide_n, stat_len)
    mean_term = (jnp.sum(stats_all[:, :tok_mlp], axis=0) / width)[:, None]
    gain_part = stats_all[:, tok_mlp : tok_mlp + cols_wide].reshape(width // 128, 128)
    resid_grad = (
        out_own.astype(jnp.float32) + inv_rms * (grad_norm * gain_own - normed_own * mean_term)
    ).astype(jnp.bfloat16)
    resid_send, grads_parts = lax.optimization_barrier((resid_grad, grads_parts))
    resid_cols, gain_all = gather([resid_send, gain_part], [("head", 0), ("head", 0)], 3)
    grad_gain = jnp.sum(gain_all.reshape(heads_n, width), axis=0)
    grad_resid = lax.all_gather(resid_grad, "wide", axis=1, tiled=True)

    tok_total = keys_all.shape[0]
    q_offset = wide_at * tok_att
    positions = jnp.arange(tok_total, dtype=jnp.int32)
    q_pos = q_offset + jnp.arange(tok_att, dtype=jnp.int32)
    q_docs = lax.dynamic_slice_in_dim(doc_ids, q_offset, tok_att, 0)
    visible = (q_docs[:, None] == doc_ids[None, :]) & (positions[None, :] <= q_pos[:, None])
    query3 = queries.reshape(tok_att, per_kv, head_dim)
    scores = (
        jnp.einsum("thd,sd->hts", query3, keys_all, preferred_element_type=jnp.float32)
        * score_scale
    )
    scores = jnp.where(visible[None], scores, -1e30)
    top = jnp.max(scores, axis=-1, keepdims=True)
    expo = jnp.exp(scores - top)
    prob = expo / jnp.sum(expo, axis=-1, keepdims=True)
    prob_b = prob.astype(jnp.bfloat16)
    attn_out = jnp.einsum("hts,sd->thd", prob_b, values_all, preferred_element_type=jnp.float32)
    attn_out = attn_out.astype(jnp.bfloat16).reshape(tok_att, per_kv * head_dim)
    attn_all = lax.all_gather(attn_out, "wide", axis=0, tiled=True)

    heads_part = jnp.dot(resid_cols, out_proj, preferred_element_type=jnp.float32)
    grad_heads = pair_scatter_sum(heads_part.astype(jnp.bfloat16), "wide", 0, 4)
    grad_heads = grad_heads.reshape(tok_att, per_kv, head_dim)
    dprob = jnp.einsum("thd,sd->hts", grad_heads, values_all, preferred_element_type=jnp.float32)
    delta = jnp.sum(prob * dprob, axis=-1, keepdims=True)
    dscore = (prob * (dprob - delta) * score_scale).astype(jnp.bfloat16)
    grad_query = jnp.einsum("hts,sd->thd", dscore, keys_all, preferred_element_type=jnp.float32)
    grad_query = grad_query.astype(jnp.bfloat16).reshape(tok_att, per_kv * head_dim)
    key_part = jnp.einsum("hts,thd->sd", dscore, query3, preferred_element_type=jnp.float32)
    value_part = jnp.einsum("hts,thd->sd", prob_b, grad_heads, preferred_element_type=jnp.float32)
    kv_sum = scatter_sum(
        jnp.concatenate([key_part, value_part], axis=1).astype(jnp.bfloat16), "wide", 0, 5
    )

    grad_proj = lax.dot_general(
        resid_cols, attn_all, contract_first, preferred_element_type=jnp.float32
    ).astype(jnp.bfloat16)
    mine = jnp.concatenate(normed_parts, axis=0)
    other = lax.ppermute(mine, "wide", [(i, i ^ 1) for i in range(wide_n)])
    normed_all = jnp.concatenate(
        [jnp.where(core == 0, mine, other), jnp.where(core == 0, other, mine)], axis=1
    )
    grads_all = jnp.concatenate(grads_parts, axis=0)
    hidden_dev = w_gate.shape[1]
    grad_gate = lax.dot_general(
        normed_all, grads_all[:, :hidden_dev], contract_first, preferred_element_type=jnp.float32
    ).astype(jnp.bfloat16)
    grad_up = lax.dot_general(
        normed_all, grads_all[:, hidden_dev:], contract_first, preferred_element_type=jnp.float32
    ).astype(jnp.bfloat16)
    return (
        grad_resid,
        grad_gain,
        grad_gate,
        grad_up,
        grad_proj,
        grad_query,
        kv_sum[:, :head_dim],
        kv_sum[:, head_dim:],
    )


def solution(mesh):
    return jax.shard_map(
        local,
        mesh=mesh,
        in_specs=(
            P("head", None),
            P(),
            P(None, "wide"),
            P(None, "wide"),
            P("head", "wide"),
            P("head", None),
            P("wide", "head"),
            P("wide", "head"),
            P("wide", "head"),
            P("wide", "head"),
            P(),
        ),
        out_specs=(
            P("head", None),
            P(),
            P("head", "wide"),
            P("head", "wide"),
            P("wide", "head"),
            P("wide", "head"),
            P("wide", "head"),
            P("wide", "head"),
        ),
        check_vma=False,
    )
```

```python
import functools
import math

import jax
import jax.numpy as jnp
from jax import lax
from jax.experimental import pallas as pl
from jax.experimental.pallas import tpu as pltpu
from jax.sharding import PartitionSpec as P

EPSILON = 1e-05
MESH = pl.DeviceIdType.MESH
ANY = pl.BlockSpec(memory_space=pl.ANY)
VMEM = pl.BlockSpec(memory_space=pltpu.VMEM)


def enter(groups):
    barrier = pltpu.get_barrier_semaphore()
    total = 0
    for axis, n in groups:
        me = lax.axis_index(axis)
        for k in range(1, n):
            pl.semaphore_signal(
                barrier, inc=1, device_id={axis: lax.rem(me + k, n)}, device_id_type=MESH
            )
        total += n - 1
    pl.semaphore_wait(barrier, total)


def part(ref, dim, index, size):
    start = pl.multiple_of(index * size, size)
    if dim == 0:
        return ref.at[pl.ds(start, size)]
    return ref.at[:, pl.ds(start, size)]


def params(collective_id):
    return pltpu.CompilerParams(
        collective_id=collective_id, has_side_effects=True, vmem_limit_bytes=32 * 1024 * 1024
    )


def scatter_sum_kernel(axis, n, dim, src, out, held, send_sem, recv_sem, own_sem):
    me = lax.axis_index(axis)
    size = out.shape[dim]
    own = pltpu.make_async_copy(part(src, dim, me, size), held.at[0], own_sem)
    own.start()
    enter([(axis, n)])
    copies = []
    for k in range(1, n):
        peer = lax.rem(me + k, n)
        copies.append(
            pltpu.make_async_remote_copy(
                src_ref=part(src, dim, peer, size),
                dst_ref=held.at[k],
                send_sem=send_sem.at[k],
                recv_sem=recv_sem.at[k],
                device_id={axis: peer},
                device_id_type=MESH,
            )
        )
        copies[-1].start()
    own.wait()
    for copy in copies:
        copy.wait()
    step = 32

    @pl.loop(0, out.shape[0] // step)
    def _(i):
        rows = pl.ds(pl.multiple_of(i * step, step), step)
        total = held[0, rows].astype(jnp.float32)
        for k in range(1, n):
            total = total + held[k, rows].astype(jnp.float32)
        out[rows] = total.astype(out.dtype)


def scatter_sum(x, axis, dim, collective_id):
    n = lax.axis_size(axis)
    shape = list(x.shape)
    shape[dim] //= n
    return pl.pallas_call(
        functools.partial(scatter_sum_kernel, axis, n, dim),
        out_shape=jax.ShapeDtypeStruct(tuple(shape), x.dtype),
        in_specs=[ANY],
        out_specs=VMEM,
        scratch_shapes=[
            pltpu.VMEM((n, *shape), x.dtype),
            pltpu.SemaphoreType.DMA((n,)),
            pltpu.SemaphoreType.DMA((n,)),
            pltpu.SemaphoreType.DMA,
        ],
        compiler_params=params(collective_id),
    )(x)


def pair_scatter_kernel(
    axis, n, dim, src, out, own, near, sums, far, near_sems, far_sems, own_sems
):
    pairs = n // 2
    me = lax.axis_index(axis)
    chip, core = me // 2, lax.rem(me, 2)
    partner = chip * 2 + 1 - core
    size = out.shape[dim]
    order = list(range(1, pairs)) + [0]
    chips = [lax.rem(chip + k, pairs) for k in range(pairs)]
    owns = {}
    for k in order:
        owns[k] = pltpu.make_async_copy(
            part(src, dim, chips[k] * 2 + core, size), own.at[k], own_sems.at[k]
        )
        owns[k].start()
    barrier = pltpu.get_barrier_semaphore()
    for k in range(pairs):
        peer = partner if k == 0 else chips[k] * 2 + core
        pl.semaphore_signal(barrier, inc=1, device_id={axis: peer}, device_id_type=MESH)
    pl.semaphore_wait(barrier, pairs)
    nears, fars = {}, {}
    for k in order:
        nears[k] = pltpu.make_async_remote_copy(
            src_ref=part(src, dim, chips[k] * 2 + 1 - core, size),
            dst_ref=near.at[k],
            send_sem=near_sems.at[0, k],
            recv_sem=near_sems.at[1, k],
            device_id={axis: partner},
            device_id_type=MESH,
        )
        nears[k].start()
    step = 32
    for k in order:
        owns[k].wait()
        nears[k].wait()
        if k == 0:
            continue

        @pl.loop(0, out.shape[0] // step)
        def _(i):
            rows = pl.ds(pl.multiple_of(i * step, step), step)
            total = own[k, rows].astype(jnp.float32) + near[k, rows].astype(jnp.float32)
            sums[k, rows] = total.astype(sums.dtype)

        fars[k] = pltpu.make_async_remote_copy(
            src_ref=sums.at[k],
            dst_ref=far.at[k],
            send_sem=far_sems.at[0, k],
            recv_sem=far_sems.at[1, k],
            device_id={axis: chips[k] * 2 + core},
            device_id_type=MESH,
        )
        fars[k].start()
    for k in range(1, pairs):
        fars[k].wait()

    @pl.loop(0, out.shape[0] // step)
    def _(i):
        rows = pl.ds(pl.multiple_of(i * step, step), step)
        total = own[0, rows].astype(jnp.float32) + near[0, rows].astype(jnp.float32)
        for k in range(1, pairs):
            total = total + far[k, rows].astype(jnp.float32)
        out[rows] = total.astype(out.dtype)


def pair_scatter_sum(x, axis, dim, collective_id):
    n = lax.axis_size(axis)
    shape = list(x.shape)
    shape[dim] //= n
    held = pltpu.VMEM((n // 2, *shape), x.dtype)
    return pl.pallas_call(
        functools.partial(pair_scatter_kernel, axis, n, dim),
        out_shape=jax.ShapeDtypeStruct(tuple(shape), x.dtype),
        in_specs=[ANY],
        out_specs=VMEM,
        scratch_shapes=[
            held,
            held,
            held,
            held,
            pltpu.SemaphoreType.DMA((2, n // 2)),
            pltpu.SemaphoreType.DMA((2, n // 2)),
            pltpu.SemaphoreType.DMA((n // 2,)),
        ],
        compiler_params=params(collective_id),
    )(x)


def gather_kernel(plan, *refs):
    count = len(plan)
    srcs, outs = refs[:count], refs[count : 2 * count]
    sems = refs[2 * count :]
    groups = []
    for axis, n, _ in plan:
        if (axis, n) not in groups:
            groups.append((axis, n))
    owns = []
    for i, (axis, n, dim) in enumerate(plan):
        me = lax.axis_index(axis)
        own = pltpu.make_async_copy(
            srcs[i], part(outs[i], dim, me, srcs[i].shape[dim]), sems[3 * i + 2]
        )
        own.start()
        owns.append(own)
    enter(groups)
    copies = []
    for i, (axis, n, dim) in enumerate(plan):
        me = lax.axis_index(axis)
        for k in range(1, n):
            copy = pltpu.make_async_remote_copy(
                src_ref=srcs[i],
                dst_ref=part(outs[i], dim, me, srcs[i].shape[dim]),
                send_sem=sems[3 * i].at[k],
                recv_sem=sems[3 * i + 1].at[k],
                device_id={axis: lax.rem(me + k, n)},
                device_id_type=MESH,
            )
            copy.start()
            copies.append(copy)
    for own in owns:
        own.wait()
    for copy in copies:
        copy.wait()


def gather(arrays, axes_dims, collective_id):
    plan, outs, scratch = [], [], []
    for x, (axis, dim) in zip(arrays, axes_dims):
        n = lax.axis_size(axis)
        plan.append((axis, n, dim))
        shape = list(x.shape)
        shape[dim] *= n
        outs.append(jax.ShapeDtypeStruct(tuple(shape), x.dtype))
        scratch += [
            pltpu.SemaphoreType.DMA((n,)),
            pltpu.SemaphoreType.DMA((n,)),
            pltpu.SemaphoreType.DMA,
        ]
    return pl.pallas_call(
        functools.partial(gather_kernel, plan),
        out_shape=outs,
        in_specs=[ANY] * len(arrays),
        out_specs=[ANY] * len(arrays),
        scratch_shapes=scratch,
        compiler_params=params(collective_id),
    )(*arrays)


def shifted(x, axis, n, k):
    return lax.ppermute(x, axis, [(i, (i + k) % n) for i in range(n)])


def local(
    residual,
    norm_gain,
    w_gate,
    w_up,
    grad_hidden,
    grad_out,
    out_proj,
    queries,
    keys_in,
    values_in,
    doc_ids,
):
    heads_n = lax.axis_size("head")
    wide_n = lax.axis_size("wide")
    head_at = lax.axis_index("head")
    wide_at = lax.axis_index("wide")
    tok_mlp, width = residual.shape
    cols_wide = width // wide_n
    cols_head = width // heads_n
    contract_last = (((1,), (1,)), ((), ()))
    contract_first = (((0,), (0,)), ((), ()))
    tok_att = queries.shape[0]
    head_dim = keys_in.shape[1]
    per_kv = queries.shape[1] // head_dim
    score_scale = 1.0 / math.sqrt(head_dim)

    keys_all, values_all = gather([keys_in, values_in], [("wide", 0), ("wide", 0)], 6)

    resid_f = residual.astype(jnp.float32)
    inv_rms = lax.rsqrt(jnp.mean(resid_f * resid_f, axis=-1, keepdims=True) + EPSILON)
    normed = (resid_f * inv_rms * norm_gain).astype(jnp.bfloat16)

    cols_piece = cols_head // wide_n

    def normed_cols(owner):
        return lax.dynamic_slice_in_dim(
            normed, owner * cols_head + wide_at * cols_piece, cols_piece, 1
        )

    normed_parts = [normed_cols(head_at)]
    for k in range(1, heads_n):
        normed_parts.append(
            shifted(normed_cols(lax.rem(head_at + k, heads_n)), "head", heads_n, k)
        )

    gate_pre = jnp.dot(normed, w_gate, preferred_element_type=jnp.float32)
    up_pre = jnp.dot(normed, w_up, preferred_element_type=jnp.float32)
    sigma = jax.nn.sigmoid(gate_pre)
    grad_h = grad_hidden.astype(jnp.float32)
    grad_g = (grad_h * up_pre * sigma * (1.0 + gate_pre * (1.0 - sigma))).astype(jnp.bfloat16)
    grad_u = (grad_h * gate_pre * sigma).astype(jnp.bfloat16)
    partial_norm = lax.dot_general(
        grad_g, w_gate, contract_last, preferred_element_type=jnp.float32
    )
    partial_norm = partial_norm + lax.dot_general(
        grad_u, w_up, contract_last, preferred_element_type=jnp.float32
    )
    gate_send, normed_parts = lax.optimization_barrier((grad_g, normed_parts))
    gate_parts = [grad_g]
    for k in range(1, heads_n):
        gate_parts.append(shifted(gate_send, "head", heads_n, k))
    normed_all = lax.all_gather(jnp.concatenate(normed_parts, axis=0), "wide", axis=0)
    grad_norm = pair_scatter_sum(partial_norm.astype(jnp.bfloat16), "wide", 1, 1)
    grad_norm = grad_norm.astype(jnp.float32)
    resid_own = lax.dynamic_slice_in_dim(residual, wide_at * cols_wide, cols_wide, 1)
    normed_own = resid_own.astype(jnp.float32) * inv_rms
    gain_own = lax.dynamic_slice_in_dim(norm_gain, wide_at * cols_wide, cols_wide, 0)
    out_own = lax.dynamic_slice_in_dim(grad_out, wide_at * cols_wide, cols_wide, 1)
    product = grad_norm * normed_own
    stats = jnp.concatenate([jnp.sum(product * gain_own, axis=1), jnp.sum(product, axis=0)])
    stat_len = -(-stats.shape[0] // 1024) * 1024
    stats = jnp.pad(stats, (0, stat_len - stats.shape[0])).reshape(stat_len // 128, 128)
    (stats_all,) = gather([stats], [("wide", 0)], 2)
    stats_all = stats_all.reshape(wide_n, stat_len)
    mean_term = (jnp.sum(stats_all[:, :tok_mlp], axis=0) / width)[:, None]
    gain_part = stats_all[:, tok_mlp : tok_mlp + cols_wide].reshape(width // 128, 128)
    resid_grad = (
        out_own.astype(jnp.float32) + inv_rms * (grad_norm * gain_own - normed_own * mean_term)
    ).astype(jnp.bfloat16)
    resid_send, gate_parts = lax.optimization_barrier((resid_grad, gate_parts))
    resid_cols, gain_all = gather([resid_send, gain_part], [("head", 0), ("head", 0)], 3)
    up_send, resid_cols = lax.optimization_barrier((grad_u, resid_cols))
    up_parts = [grad_u]
    for k in range(1, heads_n):
        up_parts.append(shifted(up_send, "head", heads_n, k))
    grad_gain = jnp.sum(gain_all.reshape(heads_n, width), axis=0)
    grad_resid = lax.all_gather(resid_grad, "wide", axis=1, tiled=True)

    tok_total = keys_all.shape[0]
    q_offset = wide_at * tok_att
    positions = jnp.arange(tok_total, dtype=jnp.int32)
    q_pos = q_offset + jnp.arange(tok_att, dtype=jnp.int32)
    q_docs = lax.dynamic_slice_in_dim(doc_ids, q_offset, tok_att, 0)
    visible = (q_docs[:, None] == doc_ids[None, :]) & (positions[None, :] <= q_pos[:, None])
    query3 = queries.reshape(tok_att, per_kv, head_dim)
    scores = (
        jnp.einsum("thd,sd->hts", query3, keys_all, preferred_element_type=jnp.float32)
        * score_scale
    )
    scores = jnp.where(visible[None], scores, -1e30)
    top = jnp.max(scores, axis=-1, keepdims=True)
    expo = jnp.exp(scores - top)
    prob = expo / jnp.sum(expo, axis=-1, keepdims=True)
    prob_b = prob.astype(jnp.bfloat16)
    attn_out = jnp.einsum("hts,sd->thd", prob_b, values_all, preferred_element_type=jnp.float32)
    attn_out = attn_out.astype(jnp.bfloat16).reshape(tok_att, per_kv * head_dim)
    attn_all = lax.all_gather(attn_out, "wide", axis=0, tiled=True)

    heads_part = jnp.dot(resid_cols, out_proj, preferred_element_type=jnp.float32)
    grad_heads = pair_scatter_sum(heads_part.astype(jnp.bfloat16), "wide", 0, 4)
    grad_heads = grad_heads.reshape(tok_att, per_kv, head_dim)
    dprob = jnp.einsum("thd,sd->hts", grad_heads, values_all, preferred_element_type=jnp.float32)
    delta = jnp.sum(prob * dprob, axis=-1, keepdims=True)
    dscore = (prob * (dprob - delta) * score_scale).astype(jnp.bfloat16)
    grad_query = jnp.einsum("hts,sd->thd", dscore, keys_all, preferred_element_type=jnp.float32)
    grad_query = grad_query.astype(jnp.bfloat16).reshape(tok_att, per_kv * head_dim)
    key_part = jnp.einsum("hts,thd->sd", dscore, query3, preferred_element_type=jnp.float32)
    value_part = jnp.einsum("hts,thd->sd", prob_b, grad_heads, preferred_element_type=jnp.float32)
    kv_sum = scatter_sum(
        jnp.concatenate([key_part, value_part], axis=1).astype(jnp.bfloat16), "wide", 0, 5
    )

    grad_proj = lax.dot_general(
        resid_cols, attn_all, contract_first, preferred_element_type=jnp.float32
    ).astype(jnp.bfloat16)
    contract_tokens = (((1,), (0,)), ((), ()))
    grad_gate, grad_up = (
        lax.dot_general(
            normed_all,
            jnp.concatenate(parts, axis=0),
            contract_tokens,
            preferred_element_type=jnp.float32,
        )
        .astype(jnp.bfloat16)
        .reshape(cols_head, -1)
        for parts in (gate_parts, up_parts)
    )
    return (
        grad_resid,
        grad_gain,
        grad_gate,
        grad_up,
        grad_proj,
        grad_query,
        kv_sum[:, :head_dim],
        kv_sum[:, head_dim:],
    )


def solution(mesh):
    return jax.shard_map(
        local,
        mesh=mesh,
        in_specs=(
            P("head", None),
            P(),
            P(None, "wide"),
            P(None, "wide"),
            P("head", "wide"),
            P("head", None),
            P("wide", "head"),
            P("wide", "head"),
            P("wide", "head"),
            P("wide", "head"),
            P(),
        ),
        out_specs=(
            P("head", None),
            P(),
            P("head", "wide"),
            P("head", "wide"),
            P("wide", "head"),
            P("wide", "head"),
            P("wide", "head"),
            P("wide", "head"),
        ),
        check_vma=False,
    )
```

```python
import functools
import math

import jax
import jax.numpy as jnp
from jax import lax
from jax.experimental import pallas as pl
from jax.experimental.pallas import tpu as pltpu
from jax.sharding import PartitionSpec as P

EPSILON = 1e-05
MESH = pl.DeviceIdType.MESH
ANY = pl.BlockSpec(memory_space=pl.ANY)
VMEM = pl.BlockSpec(memory_space=pltpu.VMEM)


def enter(groups):
    barrier = pltpu.get_barrier_semaphore()
    total = 0
    for axis, n in groups:
        me = lax.axis_index(axis)
        for k in range(1, n):
            pl.semaphore_signal(
                barrier, inc=1, device_id={axis: lax.rem(me + k, n)}, device_id_type=MESH
            )
        total += n - 1
    pl.semaphore_wait(barrier, total)


def part(ref, dim, index, size):
    start = pl.multiple_of(index * size, size)
    if dim == 0:
        return ref.at[pl.ds(start, size)]
    return ref.at[:, pl.ds(start, size)]


def moved(nbytes):
    return pl.CostEstimate(flops=0, bytes_accessed=nbytes, transcendentals=0)


def params(collective_id):
    return pltpu.CompilerParams(
        collective_id=collective_id, has_side_effects=True, vmem_limit_bytes=32 * 1024 * 1024
    )


def scatter_sum_kernel(axis, n, dim, src, out, held, send_sem, recv_sem, own_sem):
    me = lax.axis_index(axis)
    size = out.shape[dim]
    own = pltpu.make_async_copy(part(src, dim, me, size), held.at[0], own_sem)
    own.start()
    enter([(axis, n)])
    copies = []
    for k in range(1, n):
        peer = lax.rem(me + k, n)
        copies.append(
            pltpu.make_async_remote_copy(
                src_ref=part(src, dim, peer, size),
                dst_ref=held.at[k],
                send_sem=send_sem.at[k],
                recv_sem=recv_sem.at[k],
                device_id={axis: peer},
                device_id_type=MESH,
            )
        )
        copies[-1].start()
    own.wait()
    for copy in copies:
        copy.wait()
    step = 32

    @pl.loop(0, out.shape[0] // step)
    def _(i):
        rows = pl.ds(pl.multiple_of(i * step, step), step)
        total = held[0, rows].astype(jnp.float32)
        for k in range(1, n):
            total = total + held[k, rows].astype(jnp.float32)
        out[rows] = total.astype(out.dtype)


def scatter_sum(x, axis, dim, collective_id):
    n = lax.axis_size(axis)
    shape = list(x.shape)
    shape[dim] //= n
    return pl.pallas_call(
        functools.partial(scatter_sum_kernel, axis, n, dim),
        out_shape=jax.ShapeDtypeStruct(tuple(shape), x.dtype),
        in_specs=[ANY],
        out_specs=VMEM,
        scratch_shapes=[
            pltpu.VMEM((n, *shape), x.dtype),
            pltpu.SemaphoreType.DMA((n,)),
            pltpu.SemaphoreType.DMA((n,)),
            pltpu.SemaphoreType.DMA,
        ],
        compiler_params=params(collective_id),
        cost_estimate=moved(32 * x.size * x.dtype.itemsize),
    )(x)


def pair_scatter_kernel(
    axis, n, dim, src, out, own, near, sums, far, near_sems, far_sems, own_sems
):
    pairs = n // 2
    me = lax.axis_index(axis)
    chip, core = me // 2, lax.rem(me, 2)
    partner = chip * 2 + 1 - core
    size = out.shape[dim]
    order = list(range(1, pairs)) + [0]
    chips = [lax.rem(chip + k, pairs) for k in range(pairs)]
    owns = {}
    for k in order:
        owns[k] = pltpu.make_async_copy(
            part(src, dim, chips[k] * 2 + core, size), own.at[k], own_sems.at[k]
        )
        owns[k].start()
    barrier = pltpu.get_barrier_semaphore()
    for k in range(pairs):
        peer = partner if k == 0 else chips[k] * 2 + core
        pl.semaphore_signal(barrier, inc=1, device_id={axis: peer}, device_id_type=MESH)
    pl.semaphore_wait(barrier, pairs)
    nears, fars = {}, {}
    for k in order:
        nears[k] = pltpu.make_async_remote_copy(
            src_ref=part(src, dim, chips[k] * 2 + 1 - core, size),
            dst_ref=near.at[k],
            send_sem=near_sems.at[0, k],
            recv_sem=near_sems.at[1, k],
            device_id={axis: partner},
            device_id_type=MESH,
        )
        nears[k].start()
    step = 32
    for k in order:
        owns[k].wait()
        nears[k].wait()
        if k == 0:
            continue

        @pl.loop(0, out.shape[0] // step)
        def _(i):
            rows = pl.ds(pl.multiple_of(i * step, step), step)
            total = own[k, rows].astype(jnp.float32) + near[k, rows].astype(jnp.float32)
            sums[k, rows] = total.astype(sums.dtype)

        fars[k] = pltpu.make_async_remote_copy(
            src_ref=sums.at[k],
            dst_ref=far.at[k],
            send_sem=far_sems.at[0, k],
            recv_sem=far_sems.at[1, k],
            device_id={axis: chips[k] * 2 + core},
            device_id_type=MESH,
        )
        fars[k].start()
    for k in range(1, pairs):
        fars[k].wait()

    @pl.loop(0, out.shape[0] // step)
    def _(i):
        rows = pl.ds(pl.multiple_of(i * step, step), step)
        total = own[0, rows].astype(jnp.float32) + near[0, rows].astype(jnp.float32)
        for k in range(1, pairs):
            total = total + far[k, rows].astype(jnp.float32)
        out[rows] = total.astype(out.dtype)


def pair_scatter_sum(x, axis, dim, collective_id):
    n = lax.axis_size(axis)
    shape = list(x.shape)
    shape[dim] //= n
    held = pltpu.VMEM((n // 2, *shape), x.dtype)
    return pl.pallas_call(
        functools.partial(pair_scatter_kernel, axis, n, dim),
        out_shape=jax.ShapeDtypeStruct(tuple(shape), x.dtype),
        in_specs=[ANY],
        out_specs=VMEM,
        scratch_shapes=[
            held,
            held,
            held,
            held,
            pltpu.SemaphoreType.DMA((2, n // 2)),
            pltpu.SemaphoreType.DMA((2, n // 2)),
            pltpu.SemaphoreType.DMA((n // 2,)),
        ],
        compiler_params=params(collective_id),
        cost_estimate=moved(32 * x.size * x.dtype.itemsize),
    )(x)


def gather_kernel(plan, *refs):
    count = len(plan)
    srcs, outs = refs[:count], refs[count : 2 * count]
    sems = refs[2 * count :]
    groups = []
    for axis, n, _ in plan:
        if (axis, n) not in groups:
            groups.append((axis, n))
    owns = []
    for i, (axis, n, dim) in enumerate(plan):
        me = lax.axis_index(axis)
        own = pltpu.make_async_copy(
            srcs[i], part(outs[i], dim, me, srcs[i].shape[dim]), sems[3 * i + 2]
        )
        own.start()
        owns.append(own)
    enter(groups)
    copies = []
    for i, (axis, n, dim) in enumerate(plan):
        me = lax.axis_index(axis)
        for k in range(1, n):
            copy = pltpu.make_async_remote_copy(
                src_ref=srcs[i],
                dst_ref=part(outs[i], dim, me, srcs[i].shape[dim]),
                send_sem=sems[3 * i].at[k],
                recv_sem=sems[3 * i + 1].at[k],
                device_id={axis: lax.rem(me + k, n)},
                device_id_type=MESH,
            )
            copy.start()
            copies.append(copy)
    for own in owns:
        own.wait()
    for copy in copies:
        copy.wait()


def gather(arrays, axes_dims, collective_id):
    plan, outs, scratch = [], [], []
    for x, (axis, dim) in zip(arrays, axes_dims):
        n = lax.axis_size(axis)
        plan.append((axis, n, dim))
        shape = list(x.shape)
        shape[dim] *= n
        outs.append(jax.ShapeDtypeStruct(tuple(shape), x.dtype))
        scratch += [
            pltpu.SemaphoreType.DMA((n,)),
            pltpu.SemaphoreType.DMA((n,)),
            pltpu.SemaphoreType.DMA,
        ]
    return pl.pallas_call(
        functools.partial(gather_kernel, plan),
        out_shape=outs,
        in_specs=[ANY] * len(arrays),
        out_specs=[ANY] * len(arrays),
        scratch_shapes=scratch,
        compiler_params=params(collective_id),
        cost_estimate=moved(sum(96 * x.size * x.dtype.itemsize for x in arrays) + (1 << 24)),
    )(*arrays)


def shifted(x, axis, n, k):
    return lax.ppermute(x, axis, [(i, (i + k) % n) for i in range(n)])


def local(
    residual,
    norm_gain,
    w_gate,
    w_up,
    grad_hidden,
    grad_out,
    out_proj,
    queries,
    keys_in,
    values_in,
    doc_ids,
):
    heads_n = lax.axis_size("head")
    wide_n = lax.axis_size("wide")
    head_at = lax.axis_index("head")
    wide_at = lax.axis_index("wide")
    tok_mlp, width = residual.shape
    cols_wide = width // wide_n
    cols_head = width // heads_n
    contract_last = (((1,), (1,)), ((), ()))
    contract_first = (((0,), (0,)), ((), ()))
    tok_att = queries.shape[0]
    head_dim = keys_in.shape[1]
    per_kv = queries.shape[1] // head_dim
    score_scale = 1.0 / math.sqrt(head_dim)

    keys_all, values_all = gather([keys_in, values_in], [("wide", 0), ("wide", 0)], 6)

    resid_f = residual.astype(jnp.float32)
    inv_rms = lax.rsqrt(jnp.mean(resid_f * resid_f, axis=-1, keepdims=True) + EPSILON)
    normed = (resid_f * inv_rms * norm_gain).astype(jnp.bfloat16)

    cols_piece = cols_head // wide_n

    def normed_cols(owner):
        return lax.dynamic_slice_in_dim(
            normed, owner * cols_head + wide_at * cols_piece, cols_piece, 1
        )

    normed_parts = [normed_cols(head_at)]
    for k in range(1, heads_n):
        normed_parts.append(
            shifted(normed_cols(lax.rem(head_at + k, heads_n)), "head", heads_n, k)
        )

    gate_pre = jnp.dot(normed, w_gate, preferred_element_type=jnp.float32)
    up_pre = jnp.dot(normed, w_up, preferred_element_type=jnp.float32)
    sigma = jax.nn.sigmoid(gate_pre)
    grad_h = grad_hidden.astype(jnp.float32)
    grad_g = (grad_h * up_pre * sigma * (1.0 + gate_pre * (1.0 - sigma))).astype(jnp.bfloat16)
    grad_u = (grad_h * gate_pre * sigma).astype(jnp.bfloat16)
    partial_norm = lax.dot_general(
        grad_g, w_gate, contract_last, preferred_element_type=jnp.float32
    )
    partial_norm = partial_norm + lax.dot_general(
        grad_u, w_up, contract_last, preferred_element_type=jnp.float32
    )
    partial_norm, normed_parts = lax.optimization_barrier(
        (partial_norm.astype(jnp.bfloat16), normed_parts)
    )
    normed_all = lax.all_gather(jnp.concatenate(normed_parts, axis=0), "wide", axis=0)
    grad_norm = pair_scatter_sum(partial_norm, "wide", 1, 1)
    grad_norm = grad_norm.astype(jnp.float32)
    resid_own = lax.dynamic_slice_in_dim(residual, wide_at * cols_wide, cols_wide, 1)
    normed_own = resid_own.astype(jnp.float32) * inv_rms
    gain_own = lax.dynamic_slice_in_dim(norm_gain, wide_at * cols_wide, cols_wide, 0)
    out_own = lax.dynamic_slice_in_dim(grad_out, wide_at * cols_wide, cols_wide, 1)
    product = grad_norm * normed_own
    stats = jnp.concatenate([jnp.sum(product * gain_own, axis=1), jnp.sum(product, axis=0)])
    stat_len = -(-stats.shape[0] // 1024) * 1024
    stats = jnp.pad(stats, (0, stat_len - stats.shape[0])).reshape(stat_len // 128, 128)
    (stats_all,) = gather([stats], [("wide", 0)], 2)
    stats_all = stats_all.reshape(wide_n, stat_len)
    mean_term = (jnp.sum(stats_all[:, :tok_mlp], axis=0) / width)[:, None]
    gain_part = stats_all[:, tok_mlp : tok_mlp + cols_wide].reshape(width // 128, 128)
    resid_grad = (
        out_own.astype(jnp.float32) + inv_rms * (grad_norm * gain_own - normed_own * mean_term)
    ).astype(jnp.bfloat16)
    resid_cols, gain_all = gather([resid_grad, gain_part], [("head", 0), ("head", 0)], 3)
    grads_send, resid_cols = lax.optimization_barrier(
        (jnp.concatenate([grad_g, grad_u], axis=0), resid_cols)
    )
    gate_parts, up_parts = [grad_g], [grad_u]
    for k in range(1, heads_n):
        moved_in = shifted(grads_send, "head", heads_n, k)
        gate_parts.append(moved_in[:tok_mlp])
        up_parts.append(moved_in[tok_mlp:])
    grad_gain = jnp.sum(gain_all.reshape(heads_n, width), axis=0)
    grad_resid = lax.all_gather(resid_grad, "wide", axis=1, tiled=True)

    tok_total = keys_all.shape[0]
    q_offset = wide_at * tok_att
    positions = jnp.arange(tok_total, dtype=jnp.int32)
    q_pos = q_offset + jnp.arange(tok_att, dtype=jnp.int32)
    q_docs = lax.dynamic_slice_in_dim(doc_ids, q_offset, tok_att, 0)
    visible = (q_docs[:, None] == doc_ids[None, :]) & (positions[None, :] <= q_pos[:, None])
    query3 = queries.reshape(tok_att, per_kv, head_dim)
    scores = (
        jnp.einsum("thd,sd->hts", query3, keys_all, preferred_element_type=jnp.float32)
        * score_scale
    )
    scores = jnp.where(visible[None], scores, -1e30)
    top = jnp.max(scores, axis=-1, keepdims=True)
    expo = jnp.exp(scores - top)
    prob = expo / jnp.sum(expo, axis=-1, keepdims=True)
    prob_b = prob.astype(jnp.bfloat16)
    attn_out = jnp.einsum("hts,sd->thd", prob_b, values_all, preferred_element_type=jnp.float32)
    attn_out = attn_out.astype(jnp.bfloat16).reshape(tok_att, per_kv * head_dim)
    attn_all = lax.all_gather(attn_out, "wide", axis=0, tiled=True)

    heads_part = jnp.dot(resid_cols, out_proj, preferred_element_type=jnp.float32)
    grad_heads = pair_scatter_sum(heads_part.astype(jnp.bfloat16), "wide", 0, 4)
    grad_heads = grad_heads.reshape(tok_att, per_kv, head_dim)
    dprob = jnp.einsum("thd,sd->hts", grad_heads, values_all, preferred_element_type=jnp.float32)
    delta = jnp.sum(prob * dprob, axis=-1, keepdims=True)
    dscore = (prob * (dprob - delta) * score_scale).astype(jnp.bfloat16)
    grad_query = jnp.einsum("hts,sd->thd", dscore, keys_all, preferred_element_type=jnp.float32)
    grad_query = grad_query.astype(jnp.bfloat16).reshape(tok_att, per_kv * head_dim)
    key_part = jnp.einsum("hts,thd->sd", dscore, query3, preferred_element_type=jnp.float32)
    value_part = jnp.einsum("hts,thd->sd", prob_b, grad_heads, preferred_element_type=jnp.float32)
    kv_sum = scatter_sum(
        jnp.concatenate([key_part, value_part], axis=1).astype(jnp.bfloat16), "wide", 0, 5
    )

    grad_proj = lax.dot_general(
        resid_cols, attn_all, contract_first, preferred_element_type=jnp.float32
    ).astype(jnp.bfloat16)
    contract_tokens = (((1,), (0,)), ((), ()))
    grad_gate, grad_up = (
        lax.dot_general(
            normed_all,
            jnp.concatenate(parts, axis=0),
            contract_tokens,
            preferred_element_type=jnp.float32,
        )
        .astype(jnp.bfloat16)
        .reshape(cols_head, -1)
        for parts in (gate_parts, up_parts)
    )
    return (
        grad_resid,
        grad_gain,
        grad_gate,
        grad_up,
        grad_proj,
        grad_query,
        kv_sum[:, :head_dim],
        kv_sum[:, head_dim:],
    )


def solution(mesh):
    return jax.shard_map(
        local,
        mesh=mesh,
        in_specs=(
            P("head", None),
            P(),
            P(None, "wide"),
            P(None, "wide"),
            P("head", "wide"),
            P("head", None),
            P("wide", "head"),
            P("wide", "head"),
            P("wide", "head"),
            P("wide", "head"),
            P(),
        ),
        out_specs=(
            P("head", None),
            P(),
            P("head", "wide"),
            P("head", "wide"),
            P("wide", "head"),
            P("wide", "head"),
            P("wide", "head"),
            P("wide", "head"),
        ),
        check_vma=False,
    )
```
